1024 devices in a mesh: group: 32 (over z), local: 8 (over x, core), dp: 4 (over y).
Axes of the slice: x: 4, y: 4, z: 32, core: 2. Of those that a mesh axis runs over, the one named last changes fastest.
Arguments:
- tokens: bfloat16 [16384, 7168], P(('dp', 'group'), 'local'), parts along dimension 0, may hold values from -6 to 6
- group_ids: int32 [16384, 4], P(('dp', 'group')), parts along dimension 0, may hold values from 0 to 31, as said below
- send_slots: int32 [16384, 4], P(('dp', 'group')), parts along dimension 0, may hold values from 0 to 17, as said below
- routing_weights: float32 [16384, 4], P(('dp', 'group')), parts along dimension 0, may hold values from 0.1 to 1
- gate_proj: bfloat16 [32, 7168, 1024], P('group', 'local'), may hold values from -0.0625 to 0.0625
- up_proj: bfloat16 [32, 7168, 1024], P('group', 'local'), may hold values from -0.0625 to 0.0625
- down_proj: bfloat16 [32, 1024, 7168], P('group', None, 'local'), may hold values from -0.1875 to 0.1875
Outputs:
- mixed: bfloat16 [16384, 7168], P(('dp', 'group'), 'local'), parts along dimension 0
The draws below stay inside these ranges and needn't reach their ends.
There are 4 independent parts, one for each index of `dp`. The reference program is written for one: setup_inputs(seed, part) draws one part's arguments, and reference() takes and returns one part's arrays. A program takes and returns all parts, laid end to end along the dimension named above; an argument that names none is the same for every part. Nothing has to cross between parts.
Inputs may be any that keep to these rules, and one draw needn't show every extreme that they name: `group_ids`: each row names 4 different groups. In every aligned block of 128 rows no group is named by more than 18 rows; one group, the same for all blocks of a part, is named by exactly 18 rows in every block, and the numbers of rows that name each other group differ by at most one within a block. `send_slots`: within an aligned block of 128 rows, the copies that go to the same group have different slots.
All inputs are finite; a program needn't handle non-finite values.
Results may differ from the reference program's by a relative error of at most 0.029.
Values may be sent and summed in bfloat16 or wider, within the bound.
No kernel may reach another device: no remote copies, remote signals or barrier semaphores. Data moves between devices by JAX's collectives and lax.ppermute only.
A program may use at most 32 MiB of HBM per device.

```python
import math
import jax
import jax.numpy as jnp
from jax import lax

D = 7168
FFE = 1024
TOK_G = 128
TOPG = 4
SEND = 18
EXPERTS = 32
CAP = 576
TOKENS = 4096
N_GROUP = 32
N_LOCAL = 8


def routing(key):
    hot_group = jax.random.randint(jax.random.fold_in(key, 11), (), 0, N_GROUP).astype(jnp.int32)
    block_keys = jax.random.split(jax.random.fold_in(key, 12), N_GROUP)
    others_count = N_GROUP - 1
    hot_rows = SEND

    def one_block(block_key):
        first_key, second_key, third_key, fourth_key = jax.random.split(block_key, 4)
        shuffled = jax.random.permutation(first_key, others_count).astype(jnp.int32)
        others = shuffled + (shuffled >= hot_group).astype(jnp.int32)
        order = jax.random.permutation(second_key, TOK_G).astype(jnp.int32)
        is_hot = (order < hot_rows).astype(jnp.int32)
        offsets = jnp.where(is_hot == 1, order * (TOPG - 1), hot_rows * (TOPG - 1) + (order - hot_rows) * TOPG)
        columns = jnp.arange(TOPG, dtype=jnp.int32)
        position = (offsets[:, None] + columns[None, :] - is_hot[:, None]) % others_count
        chosen = others[position]
        chosen = jnp.where((columns[None, :] == 0) & (is_hot[:, None] == 1), hot_group, chosen)
        turns = jax.random.randint(third_key, (TOK_G, 1), 0, TOPG).astype(jnp.int32)
        chosen = jnp.take_along_axis(chosen, (columns[None, :] + turns) % TOPG, axis=1)
        priority = jax.random.permutation(fourth_key, TOK_G).astype(jnp.int32)
        all_groups = jnp.arange(N_GROUP, dtype=jnp.int32)
        member = jnp.any(chosen[:, :, None] == all_groups[None, None, :], axis=1).astype(jnp.int32)
        earlier = (priority[None, :] < priority[:, None]).astype(jnp.int32)
        below = jnp.sum(earlier[:, :, None] * member[None, :, :], axis=1)
        slots = jnp.take_along_axis(below, chosen, axis=1)
        return (chosen, slots)
    chosen, slots = jax.vmap(one_block)(block_keys)
    return (chosen.reshape(TOKENS, TOPG).astype(jnp.int32), slots.reshape(TOKENS, TOPG).astype(jnp.int32))


def draw_group_ids(key, part):
    chosen, slots = routing(key)
    return chosen


def draw_send_slots(key, part):
    chosen, slots = routing(key)
    return slots


def block_scale(key, shape, shards, low, largest):
    factor_of = 1.0
    for axis_at, blocks in shards:
        draws = jax.random.uniform(jax.random.fold_in(jax.random.fold_in(key, 6), axis_at), (blocks,), jnp.float32, low / len(shards), largest / len(shards))
        factor_of = factor_of * jnp.repeat(jnp.exp(draws), shape[axis_at] // blocks).reshape((-1,) + (1,) * (len(shape) - 1 - axis_at))
    return factor_of


def scatter_about(rng, extent, deviation, limit, cuts=(), held_as=jnp.bfloat16):
    result = deviation * jax.random.normal(rng, extent, jnp.float32)
    if cuts:
        result = result * block_scale(rng, extent, cuts, -0.22, 0.18)
    return jnp.clip(result, -limit, limit).astype(held_as)


def setup_inputs(seed: int = 0, part: int = 0) -> dict:
    seeds = jax.random.split(jax.random.key(seed), 8)
    part_splits = jax.random.split(jax.random.fold_in(seeds[7], part), 8)
    return {
        "tokens": scatter_about(part_splits[0], (TOKENS, D), 1.0, 6.0, ((0, 32), (1, 8))),
        "group_ids": draw_group_ids(jax.random.fold_in(jax.random.fold_in(seeds[7], part), 71), part),
        "send_slots": draw_send_slots(jax.random.fold_in(jax.random.fold_in(seeds[7], part), 71), part),
        "routing_weights": jnp.clip(jnp.exp(math.log(1.0) - 2.3025851 * jax.random.uniform(part_splits[3], (TOKENS, TOPG), jnp.float32) ** block_scale(part_splits[3], (TOKENS, TOPG), ((0, 32),), -0.2, 0.2)), 0.1, 1.0),
        "gate_proj": scatter_about(seeds[4], (EXPERTS, D, FFE), D ** -0.5, 0.0625, ((0, 32), (1, 8))),
        "up_proj": scatter_about(seeds[5], (EXPERTS, D, FFE), D ** -0.5, 0.0625, ((0, 32), (1, 8))),
        "down_proj": scatter_about(seeds[6], (EXPERTS, FFE, D), FFE ** -0.5, 0.1875, ((0, 32), (2, 8))),
    }


def reference(tokens, group_ids, send_slots, routing_weights, gate_proj, up_proj, down_proj):
    feature_rows = D // N_LOCAL
    blocks = jnp.arange(TOKENS, dtype=jnp.int32) // TOK_G
    buffer_rows = (blocks[:, None] * SEND + send_slots).astype(jnp.int32)

    def block_sum(arrived, weights):
        pieces = arrived.reshape(CAP, N_LOCAL, feature_rows).astype(jnp.float32)
        parts = weights.reshape(N_LOCAL, feature_rows, FFE).astype(jnp.float32)
        partial_value = jnp.einsum('cnd,ndf->ncf', pieces, parts)
        rounded = lax.optimization_barrier(partial_value.astype(jnp.bfloat16))
        return jnp.sum(rounded.astype(jnp.float32), axis=0)

    def expert(index):
        match = group_ids == index
        target = jnp.where(match, buffer_rows, CAP)
        place = jnp.min(target, axis=1).astype(jnp.int32)
        arrived = jnp.zeros((CAP + 1, D), jnp.bfloat16).at[place].set(tokens)[:CAP]
        gate_pre = block_sum(arrived, gate_proj[index])
        up_pre = block_sum(arrived, up_proj[index])
        hidden = (jax.nn.silu(gate_pre) * up_pre).astype(jnp.bfloat16)
        return jnp.dot(hidden, down_proj[index], preferred_element_type=jnp.float32).astype(jnp.bfloat16)

    expert_out = lax.map(expert, jnp.arange(EXPERTS, dtype=jnp.int32))
    picked = expert_out[group_ids, buffer_rows].astype(jnp.float32)
    mixed = jnp.sum(routing_weights[:, :, None] * picked, axis=1)
    return mixed.astype(jnp.bfloat16)
```

```python
import jax
import jax.numpy as jnp
from jax import lax
from jax.sharding import PartitionSpec as P

LANES = 128
BASE = 16


def on_device(tokens, group_ids, send_slots, routing_weights, gate_proj, up_proj, down_proj, n_chunks=2):
    f32, bf16 = jnp.float32, jnp.bfloat16
    groups = lax.axis_size("group")
    n_local = lax.axis_size("local")
    n_x = n_local // 2
    tok_rows, feats = tokens.shape
    hidden_size = gate_proj.shape[2]
    share = hidden_size // n_local
    half = hidden_size // 2
    where = lax.axis_index("local")
    core, at_x = where % 2, where // 2

    ids_t = group_ids.T
    group_iota = jnp.arange(groups, dtype=jnp.int32)
    named = ids_t[:, None, :] == group_iota[None, :, None]
    member = jnp.any(named, axis=0)
    weight_of = jnp.sum(jnp.where(named, routing_weights.T[:, None, :], 0.0), axis=0)
    before = jnp.arange(tok_rows)[:, None] < jnp.arange(tok_rows)[None, :]
    rank = jnp.dot(member.astype(bf16), before.astype(bf16), preferred_element_type=f32)
    rank = jnp.where(member, rank, -1.0).astype(jnp.int32)

    def rows_of(first, count):
        slots = first + jnp.arange(count, dtype=jnp.int32)
        match = rank[:, None, :] == slots[None, :, None]
        mixing = jnp.where(match, weight_of[:, None, :], 0.0)
        return match.reshape(groups * count, tok_rows), mixing.reshape(groups * count, tok_rows)

    def pick(match):
        return jnp.dot(match.astype(bf16), tokens, preferred_element_type=f32).astype(bf16)

    tiles = feats // LANES
    n_extra = 2
    extra_cols = -(-n_extra * tiles // 8)

    def pack(rows, per):
        a = rows.reshape(-1, n_extra * tiles, LANES)
        a = jnp.pad(a, ((0, 0), (0, per * ((n_extra * tiles + per - 1) // per) - n_extra * tiles), (0, 0)))
        k = a.shape[1] // per
        return a.reshape(-1, k, per, LANES).transpose(0, 2, 1, 3).reshape(-1, per, k * LANES)

    def unpack(block, per):
        k = block.shape[2] // LANES
        a = block.reshape(-1, per, k, LANES).transpose(0, 2, 1, 3).reshape(-1, k * per, LANES)
        return a[:, : n_extra * tiles].reshape(-1, feats)

    def order(w, axis, side):
        return [
            lax.dynamic_slice_in_dim(w, side * half + ((at_x + j) % n_x) * share, share, axis)
            for j in range(n_x)
        ]

    def both(side):
        cols = []
        for g, u in zip(order(gate_proj[0], 1, side), order(up_proj[0], 1, side)):
            cols += [g, u]
        return jnp.concatenate(cols, axis=1)

    w_other, w_mine = both(1 - core), both(core)
    d_mine = jnp.concatenate(order(down_proj[0], 0, core), axis=0)
    d_other = jnp.concatenate(order(down_proj[0], 0, 1 - core), axis=0)

    pair = [(i, i ^ 1) for i in range(n_local)]

    def x_shift(j):
        return [(i, ((i // 2 + j) % n_x) * 2 + i % 2) for i in range(n_local)]

    def a2a(v):
        return lax.all_to_all(v, "group", split_axis=0, concat_axis=0, tiled=True)

    def expert(arrived):
        other = jnp.dot(arrived, w_other, preferred_element_type=f32).astype(bf16)
        got = lax.ppermute(other, "local", pair)
        mine = jnp.dot(arrived, w_mine, preferred_element_type=f32).astype(bf16)
        total = mine.astype(f32) + got.astype(f32)
        width = 2 * share
        parts = [total[:, j * width : (j + 1) * width] for j in range(n_x)]
        came = [lax.ppermute(parts[j].astype(bf16), "local", x_shift(j)) for j in (2, 1, 3)]
        pre = parts[0] + sum(v.astype(f32) for v in came)
        hidden = (jax.nn.silu(pre[:, :share]) * pre[:, share:]).astype(bf16)
        shares = [hidden] + [None] * (n_x - 1)
        for j in (2, 1, 3):
            shares[j] = lax.ppermute(hidden, "local", x_shift(-j))
        hidden_mine = jnp.concatenate(shares, axis=1)
        hidden_other = lax.ppermute(hidden_mine, "local", pair)
        out = jnp.dot(hidden_mine, d_mine, preferred_element_type=f32) + jnp.dot(
            hidden_other, d_other, preferred_element_type=f32
        )
        return out.astype(bf16)

    per = BASE // n_chunks
    extra_match, extra_mixing = rows_of(BASE, n_extra)
    hot = jnp.any(rank >= BASE, axis=1)
    extra_rows = pick(jnp.any(extra_match.reshape(groups, n_extra, tok_rows), axis=0))
    extra_tile = pack(extra_rows, per)
    extra_send = jnp.where(hot[:, None, None], extra_tile, jnp.zeros((), bf16))

    arrivals = []
    mixings = []
    for k in range(n_chunks):
        match, mixing = rows_of(k * per, per)
        outgoing = pick(match).reshape(groups, per, feats)
        if k == n_chunks - 1:
            outgoing = jnp.concatenate([outgoing, extra_send], axis=2)
        arrivals.append(a2a(outgoing))
        mixings.append(mixing)

    mixed = None
    for k in range(n_chunks):
        got = arrivals[k]
        last = k == n_chunks - 1
        rows = got[:, :, :feats].reshape(groups * per, feats)
        if last:
            rows = jnp.concatenate([rows, unpack(got[:, :, feats:], per)], axis=0)
        out = expert(rows)
        back = out[: groups * per].reshape(groups, per, feats)
        if last:
            back = jnp.concatenate([back, pack(out[groups * per :], per)], axis=2)
        back = a2a(back)
        mixing = mixings[k]
        rows = back[:, :, :feats].reshape(groups * per, feats)
        if last:
            rows = jnp.concatenate([rows, unpack(back[:, :, feats:], per)], axis=0)
            mixing = jnp.concatenate([mixing, extra_mixing], axis=0)
        part = jnp.einsum("ct,cd->td", mixing, rows.astype(f32), precision=lax.Precision.HIGHEST)
        mixed = part if mixed is None else mixed + part
    return mixed.astype(bf16)


def solution(mesh):
    return jax.shard_map(
        on_device,
        mesh=mesh,
        in_specs=(
            P(("dp", "group"), "local"),
            P(("dp", "group"), None),
            P(("dp", "group"), None),
            P(("dp", "group"), None),
            P("group", "local", None),
            P("group", "local", None),
            P("group", None, "local"),
        ),
        out_specs=P(("dp", "group"), "local"),
        check_vma=False,
    )
```

```python
import jax
import jax.numpy as jnp
from jax import lax
from jax.sharding import PartitionSpec as P

LANES = 128
BASE = 16


def on_device(tokens, group_ids, send_slots, routing_weights, gate_proj, up_proj, down_proj, n_chunks=1):
    f32, bf16 = jnp.float32, jnp.bfloat16
    groups = lax.axis_size("group")
    n_local = lax.axis_size("local")
    n_x = n_local // 2
    tok_rows, feats = tokens.shape
    hidden_size = gate_proj.shape[2]
    share = hidden_size // n_local
    half = hidden_size // 2
    where = lax.axis_index("local")
    core = where % 2

    ids_t = group_ids.T
    group_iota = jnp.arange(groups, dtype=jnp.int32)
    named = ids_t[:, None, :] == group_iota[None, :, None]
    member = jnp.any(named, axis=0)
    weight_of = jnp.sum(jnp.where(named, routing_weights.T[:, None, :], 0.0), axis=0)
    before = jnp.arange(tok_rows)[:, None] < jnp.arange(tok_rows)[None, :]
    rank = jnp.dot(member.astype(bf16), before.astype(bf16), preferred_element_type=f32)
    rank = jnp.where(member, rank, -1.0).astype(jnp.int32)

    def rows_of(first, count):
        slots = first + jnp.arange(count, dtype=jnp.int32)
        match = rank[:, None, :] == slots[None, :, None]
        mixing = jnp.where(match, weight_of[:, None, :], 0.0)
        return match.reshape(groups * count, tok_rows), mixing.reshape(groups * count, tok_rows)

    def pick(match):
        return jnp.dot(match.astype(bf16), tokens, preferred_element_type=f32).astype(bf16)

    tiles = feats // LANES
    n_extra = 2
    extra_cols = -(-n_extra * tiles // 8)

    def pack(rows, per):
        a = rows.reshape(-1, n_extra * tiles, LANES)
        a = jnp.pad(a, ((0, 0), (0, per * ((n_extra * tiles + per - 1) // per) - n_extra * tiles), (0, 0)))
        k = a.shape[1] // per
        return a.reshape(-1, k, per, LANES).transpose(0, 2, 1, 3).reshape(-1, per, k * LANES)

    def unpack(block, per):
        k = block.shape[2] // LANES
        a = block.reshape(-1, per, k, LANES).transpose(0, 2, 1, 3).reshape(-1, k * per, LANES)
        return a[:, : n_extra * tiles].reshape(-1, feats)

    def order(w, axis, side):
        return [
            lax.dynamic_slice_in_dim(w, side * half + j * share, share, axis)
            for j in range(n_x)
        ]

    def both(side):
        cols = []
        for g, u in zip(order(gate_proj[0], 1, side), order(up_proj[0], 1, side)):
            cols += [g, u]
        return jnp.concatenate(cols, axis=1)

    w_other, w_mine = both(1 - core), both(core)
    d_mine = jnp.concatenate(order(down_proj[0], 0, core), axis=0)
    d_other = jnp.concatenate(order(down_proj[0], 0, 1 - core), axis=0)

    pair = [(i, i ^ 1) for i in range(n_local)]

    rings = [[2 * i + c for i in range(n_x)] for c in range(2)]

    def x_all(v):
        return lax.all_to_all(v, "local", split_axis=0, concat_axis=0, tiled=True, axis_index_groups=rings)

    def a2a(v):
        return lax.all_to_all(v, "group", split_axis=0, concat_axis=0, tiled=True)

    def expert(arrived):
        other = jnp.dot(arrived, w_other, preferred_element_type=f32).astype(bf16)
        got = lax.ppermute(other, "local", pair)
        mine = jnp.dot(arrived, w_mine, preferred_element_type=f32).astype(bf16)
        total = mine.astype(f32) + got.astype(f32)
        width = 2 * share
        parts = jnp.stack([total[:, j * width : (j + 1) * width] for j in range(n_x)])
        pre = jnp.sum(x_all(parts.astype(bf16)).astype(f32), axis=0)
        hidden = (jax.nn.silu(pre[:, :share]) * pre[:, share:]).astype(bf16)
        shares = x_all(jnp.broadcast_to(hidden[None], (n_x,) + hidden.shape))
        hidden_mine = jnp.concatenate([shares[j] for j in range(n_x)], axis=1)
        hidden_other = lax.ppermute(hidden_mine, "local", pair)
        out = jnp.dot(hidden_mine, d_mine, preferred_element_type=f32) + jnp.dot(
            hidden_other, d_other, preferred_element_type=f32
        )
        return out.astype(bf16)

    def mix(mixing, rows):
        out = None
        left = mixing
        for _ in range(3):
            term = lax.reduce_precision(left, 8, 7)
            left = left - term
            part = jnp.einsum("ct,cd->td", term.astype(bf16), rows, preferred_element_type=f32)
            out = part if out is None else out + part
        return out

    per = BASE // n_chunks
    extra_match, extra_mixing = rows_of(BASE, n_extra)
    hot = jnp.any(rank >= BASE, axis=1)
    extra_rows = pick(jnp.any(extra_match.reshape(groups, n_extra, tok_rows), axis=0))
    extra_tile = pack(extra_rows, per)
    extra_send = jnp.where(hot[:, None, None], extra_tile, jnp.zeros((), bf16))

    arrivals = []
    mixings = []
    for k in range(n_chunks):
        match, mixing = rows_of(k * per, per)
        outgoing = pick(match).reshape(groups, per, feats)
        if k == n_chunks - 1:
            outgoing = jnp.concatenate([outgoing, extra_send], axis=2)
        arrivals.append(a2a(outgoing))
        mixings.append(mixing)

    returned = []
    sent = None
    for k in range(n_chunks):
        got = arrivals[k]
        last = k == n_chunks - 1
        if sent is not None:
            got, sent = lax.optimization_barrier((got, sent))
            returned.append(a2a(sent))
        rows = got[:, :, :feats].reshape(groups * per, feats)
        if last:
            rows = jnp.concatenate([rows, unpack(got[:, :, feats:], per)], axis=0)
        out = expert(rows)
        sent = out[: groups * per].reshape(groups, per, feats)
        if last:
            sent = jnp.concatenate([sent, pack(out[groups * per :], per)], axis=2)
    returned.append(a2a(sent))

    mixed = None
    for k in range(n_chunks):
        back, mixing = returned[k], mixings[k]
        rows = back[:, :, :feats].reshape(groups * per, feats)
        if k == n_chunks - 1:
            rows = jnp.concatenate([rows, unpack(back[:, :, feats:], per)], axis=0)
            mixing = jnp.concatenate([mixing, extra_mixing], axis=0)
        part = mix(mixing, rows)
        mixed = part if mixed is None else mixed + part
    return mixed.astype(bf16)


def solution(mesh):
    return jax.shard_map(
        on_device,
        mesh=mesh,
        in_specs=(
            P(("dp", "group"), "local"),
            P(("dp", "group"), None),
            P(("dp", "group"), None),
            P(("dp", "group"), None),
            P("group", "local", None),
            P("group", "local", None),
            P("group", None, "local"),
        ),
        out_specs=P(("dp", "group"), "local"),
        check_vma=False,
    )
```

```python
import jax
import jax.numpy as jnp
from jax import lax
from jax.sharding import PartitionSpec as P

LANES = 128
BASE = 16


def on_device(tokens, group_ids, send_slots, routing_weights, gate_proj, up_proj, down_proj, n_chunks=1):
    f32, bf16 = jnp.float32, jnp.bfloat16
    groups = lax.axis_size("group")
    n_local = lax.axis_size("local")
    n_x = n_local // 2
    tok_rows, feats = tokens.shape
    hidden_size = gate_proj.shape[2]
    share = hidden_size // n_local
    half = hidden_size // 2
    where = lax.axis_index("local")
    core = where % 2

    ids_t = group_ids.T
    peers = [i // 2 + (i % 2) * (groups // 2) for i in range(groups)]
    group_iota = jnp.array(peers, dtype=jnp.int32)
    named = ids_t[:, None, :] == group_iota[None, :, None]
    member = jnp.any(named, axis=0)
    weight_of = jnp.sum(jnp.where(named, routing_weights.T[:, None, :], 0.0), axis=0)
    before = jnp.arange(tok_rows)[:, None] < jnp.arange(tok_rows)[None, :]
    rank = jnp.dot(member.astype(bf16), before.astype(bf16), preferred_element_type=f32)
    rank = jnp.where(member, rank, -1.0).astype(jnp.int32)

    def rows_of(first, count):
        slots = first + jnp.arange(count, dtype=jnp.int32)
        match = rank[:, None, :] == slots[None, :, None]
        mixing = jnp.where(match, weight_of[:, None, :], 0.0)
        return match.reshape(groups * count, tok_rows), mixing.reshape(groups * count, tok_rows)

    def pick(match):
        return jnp.dot(match.astype(bf16), tokens, preferred_element_type=f32).astype(bf16)

    tiles = feats // LANES
    n_extra = 2
    extra_cols = -(-n_extra * tiles // 8)

    def pack(rows, per):
        a = rows.reshape(-1, n_extra * tiles, LANES)
        a = jnp.pad(a, ((0, 0), (0, per * ((n_extra * tiles + per - 1) // per) - n_extra * tiles), (0, 0)))
        k = a.shape[1] // per
        return a.reshape(-1, k, per, LANES).transpose(0, 2, 1, 3).reshape(-1, per, k * LANES)

    def unpack(block, per):
        k = block.shape[2] // LANES
        a = block.reshape(-1, per, k, LANES).transpose(0, 2, 1, 3).reshape(-1, k * per, LANES)
        return a[:, : n_extra * tiles].reshape(-1, feats)

    def order(w, axis, side):
        return [
            lax.dynamic_slice_in_dim(w, side * half + j * share, share, axis)
            for j in range(n_x)
        ]

    def both(side):
        cols = []
        for g, u in zip(order(gate_proj[0], 1, side), order(up_proj[0], 1, side)):
            cols += [g, u]
        return jnp.concatenate(cols, axis=1)

    w_other, w_mine = both(1 - core), both(core)
    d_mine = jnp.concatenate(order(down_proj[0], 0, core), axis=0)
    d_other = jnp.concatenate(order(down_proj[0], 0, 1 - core), axis=0)

    pair = [(i, i ^ 1) for i in range(n_local)]

    rings = [[2 * i + c for i in range(n_x)] for c in range(2)]

    def x_all(v):
        return lax.all_to_all(v, "local", split_axis=0, concat_axis=0, tiled=True, axis_index_groups=rings)

    def a2a(v):
        return lax.all_to_all(v, "group", split_axis=0, concat_axis=0, tiled=True, axis_index_groups=[peers])

    def expert(arrived):
        other = jnp.dot(arrived, w_other, preferred_element_type=f32).astype(bf16)
        got = lax.ppermute(other, "local", pair)
        mine = jnp.dot(arrived, w_mine, preferred_element_type=f32).astype(bf16)
        total = mine.astype(f32) + got.astype(f32)
        width = 2 * share
        parts = jnp.stack([total[:, j * width : (j + 1) * width] for j in range(n_x)])
        pre = jnp.sum(x_all(parts.astype(bf16)).astype(f32), axis=0)
        hidden = (jax.nn.silu(pre[:, :share]) * pre[:, share:]).astype(bf16)
        shares = x_all(jnp.broadcast_to(hidden[None], (n_x,) + hidden.shape))
        hidden_mine = jnp.concatenate([shares[j] for j in range(n_x)], axis=1)
        hidden_other = lax.ppermute(hidden_mine, "local", pair)
        out = jnp.dot(hidden_mine, d_mine, preferred_element_type=f32) + jnp.dot(
            hidden_other, d_other, preferred_element_type=f32
        )
        return out.astype(bf16)

    def mix(mixing, rows):
        out = None
        left = mixing
        for _ in range(3):
            term = lax.reduce_precision(left, 8, 7)
            left = left - term
            part = jnp.einsum("ct,cd->td", term.astype(bf16), rows, preferred_element_type=f32)
            out = part if out is None else out + part
        return out

    per = BASE // n_chunks
    extra_match, extra_mixing = rows_of(BASE, n_extra)
    hot = jnp.any(rank >= BASE, axis=1)
    extra_rows = pick(jnp.any(extra_match.reshape(groups, n_extra, tok_rows), axis=0))
    extra_tile = pack(extra_rows, per)
    extra_send = jnp.where(hot[:, None, None], extra_tile, jnp.zeros((), bf16))

    arrivals = []
    mixings = []
    for k in range(n_chunks):
        match, mixing = rows_of(k * per, per)
        outgoing = pick(match).reshape(groups, per, feats)
        if k == n_chunks - 1:
            outgoing = jnp.concatenate([outgoing, extra_send], axis=2)
        arrivals.append(a2a(outgoing))
        mixings.append(mixing)

    returned = []
    sent = None
    for k in range(n_chunks):
        got = arrivals[k]
        last = k == n_chunks - 1
        if sent is not None:
            got, sent = lax.optimization_barrier((got, sent))
            returned.append(a2a(sent))
        rows = got[:, :, :feats].reshape(groups * per, feats)
        if last:
            rows = jnp.concatenate([rows, unpack(got[:, :, feats:], per)], axis=0)
        out = expert(rows)
        sent = out[: groups * per].reshape(groups, per, feats)
        if last:
            sent = jnp.concatenate([sent, pack(out[groups * per :], per)], axis=2)
    returned.append(a2a(sent))

    mixed = None
    for k in range(n_chunks):
        back, mixing = returned[k], mixings[k]
        rows = back[:, :, :feats].reshape(groups * per, feats)
        if k == n_chunks - 1:
            rows = jnp.concatenate([rows, unpack(back[:, :, feats:], per)], axis=0)
            mixing = jnp.concatenate([mixing, extra_mixing], axis=0)
        part = mix(mixing, rows)
        mixed = part if mixed is None else mixed + part
    return mixed.astype(bf16)


def solution(mesh):
    return jax.shard_map(
        on_device,
        mesh=mesh,
        in_specs=(
            P(("dp", "group"), "local"),
            P(("dp", "group"), None),
            P(("dp", "group"), None),
            P(("dp", "group"), None),
            P("group", "local", None),
            P("group", "local", None),
            P("group", None, "local"),
        ),
        out_specs=P(("dp", "group"), "local"),
        check_vma=False,
    )
```

```python
import jax
import jax.numpy as jnp
from jax import lax
from jax.sharding import PartitionSpec as P

LANES = 128
BASE = 16


def on_device(tokens, group_ids, send_slots, routing_weights, gate_proj, up_proj, down_proj, n_chunks=1):
    f32, bf16 = jnp.float32, jnp.bfloat16
    groups = lax.axis_size("group")
    n_local = lax.axis_size("local")
    n_x = n_local // 2
    tok_rows, feats = tokens.shape
    hidden_size = gate_proj.shape[2]
    share = hidden_size // n_local
    half = hidden_size // 2
    where = lax.axis_index("local")
    core = where % 2

    ids_t = group_ids.T
    peers = [i // 2 + (i % 2) * (groups // 2) for i in range(groups)]
    group_iota = jnp.array(peers, dtype=jnp.int32)
    named = ids_t[:, None, :] == group_iota[None, :, None]
    member = jnp.any(named, axis=0)
    weight_of = jnp.sum(jnp.where(named, routing_weights.T[:, None, :], 0.0), axis=0)
    before = jnp.arange(tok_rows)[:, None] < jnp.arange(tok_rows)[None, :]
    rank = jnp.dot(member.astype(bf16), before.astype(bf16), preferred_element_type=f32)
    rank = jnp.where(member, rank, -1.0).astype(jnp.int32)

    def rows_of(first, count):
        slots = first + jnp.arange(count, dtype=jnp.int32)
        match = rank[:, None, :] == slots[None, :, None]
        mixing = jnp.where(match, weight_of[:, None, :], 0.0)
        return match.reshape(groups * count, tok_rows), mixing.reshape(groups * count, tok_rows)

    def pick(match):
        return jnp.dot(match.astype(bf16), tokens, preferred_element_type=f32).astype(bf16)

    tiles = feats // LANES
    n_extra = 2
    extra_cols = -(-n_extra * tiles // 8)

    def pack(rows, per):
        a = rows.reshape(-1, n_extra * tiles, LANES)
        a = jnp.pad(a, ((0, 0), (0, per * ((n_extra * tiles + per - 1) // per) - n_extra * tiles), (0, 0)))
        k = a.shape[1] // per
        return a.reshape(-1, k, per, LANES).transpose(0, 2, 1, 3).reshape(-1, per, k * LANES)

    def unpack(block, per):
        k = block.shape[2] // LANES
        a = block.reshape(-1, per, k, LANES).transpose(0, 2, 1, 3).reshape(-1, k * per, LANES)
        return a[:, : n_extra * tiles].reshape(-1, feats)

    def order(w, axis, side):
        return [
            lax.dynamic_slice_in_dim(w, side * half + j * share, share, axis)
            for j in range(n_x)
        ]

    def both(side):
        cols = []
        for g, u in zip(order(gate_proj[0], 1, side), order(up_proj[0], 1, side)):
            cols += [g, u]
        return jnp.concatenate(cols, axis=1)

    w_other, w_mine = both(1 - core), both(core)
    d_mine = jnp.concatenate(order(down_proj[0], 0, core), axis=0)
    d_other = jnp.concatenate(order(down_proj[0], 0, 1 - core), axis=0)

    pair = [(i, i ^ 1) for i in range(n_local)]

    rings = [[2 * i + c for i in range(n_x)] for c in range(2)]

    def x_all(v):
        return lax.all_to_all(v, "local", split_axis=0, concat_axis=0, tiled=True, axis_index_groups=rings)

    def a2a(v):
        return lax.all_to_all(v, "group", split_axis=0, concat_axis=0, tiled=True, axis_index_groups=[peers])

    def expert(arrived):
        other = jnp.dot(arrived, w_other, preferred_element_type=f32).astype(bf16)
        got = lax.ppermute(other, "local", pair)
        mine = jnp.dot(arrived, w_mine, preferred_element_type=f32).astype(bf16)
        total = mine.astype(f32) + got.astype(f32)
        width = 2 * share
        parts = jnp.stack([total[:, j * width : (j + 1) * width] for j in range(n_x)])
        pre = jnp.sum(x_all(parts.astype(bf16)).astype(f32), axis=0)
        hidden = (jax.nn.silu(pre[:, :share]) * pre[:, share:]).astype(bf16)
        shares = x_all(jnp.broadcast_to(hidden[None], (n_x,) + hidden.shape))
        hidden_mine = jnp.concatenate([shares[j] for j in range(n_x)], axis=1)
        hidden_other = lax.ppermute(hidden_mine, "local", pair)
        out = jnp.dot(hidden_mine, d_mine, preferred_element_type=f32) + jnp.dot(
            hidden_other, d_other, preferred_element_type=f32
        )
        return out.astype(bf16)

    def mix(mixing, rows):
        terms, left = [], mixing
        for _ in range(3):
            terms.append(lax.reduce_precision(left, 8, 7))
            left = left - terms[-1]
        split = jnp.concatenate(terms, axis=1).astype(bf16)
        parts = jnp.einsum("cs,cd->sd", split, rows, preferred_element_type=f32)
        return parts[:tok_rows] + parts[tok_rows : 2 * tok_rows] + parts[2 * tok_rows :]

    per = BASE // n_chunks
    extra_match, extra_mixing = rows_of(BASE, n_extra)
    hot = jnp.any(rank >= BASE, axis=1)
    extra_rows = pick(jnp.any(extra_match.reshape(groups, n_extra, tok_rows), axis=0))
    extra_tile = pack(extra_rows, per)
    extra_send = jnp.where(hot[:, None, None], extra_tile, jnp.zeros((), bf16))

    arrivals = []
    mixings = []
    for k in range(n_chunks):
        match, mixing = rows_of(k * per, per)
        outgoing = pick(match).reshape(groups, per, feats)
        if k == n_chunks - 1:
            outgoing = jnp.concatenate([outgoing, extra_send], axis=2)
        arrivals.append(a2a(outgoing))
        mixings.append(mixing)

    returned = []
    sent = None
    for k in range(n_chunks):
        got = arrivals[k]
        last = k == n_chunks - 1
        if sent is not None:
            got, sent = lax.optimization_barrier((got, sent))
            returned.append(a2a(sent))
        rows = got[:, :, :feats].reshape(groups * per, feats)
        if last:
            rows = jnp.concatenate([rows, unpack(got[:, :, feats:], per)], axis=0)
        out = expert(rows)
        sent = out[: groups * per].reshape(groups, per, feats)
        if last:
            sent = jnp.concatenate([sent, pack(out[groups * per :], per)], axis=2)
    returned.append(a2a(sent))

    mixed = None
    for k in range(n_chunks):
        back, mixing = returned[k], mixings[k]
        rows = back[:, :, :feats].reshape(groups * per, feats)
        if k == n_chunks - 1:
            rows = jnp.concatenate([rows, unpack(back[:, :, feats:], per)], axis=0)
            mixing = jnp.concatenate([mixing, extra_mixing], axis=0)
        part = mix(mixing, rows)
        mixed = part if mixed is None else mixed + part
    return mixed.astype(bf16)


def solution(mesh):
    return jax.shard_map(
        on_device,
        mesh=mesh,
        in_specs=(
            P(("dp", "group"), "local"),
            P(("dp", "group"), None),
            P(("dp", "group"), None),
            P(("dp", "group"), None),
            P("group", "local", None),
            P("group", "local", None),
            P("group", None, "local"),
        ),
        out_specs=P(("dp", "group"), "local"),
        check_vma=False,
    )
```
